256 devices in a mesh: sec: 32 (over z, x), op: 8 (over y, core).
Axes of the slice: x: 4, y: 4, z: 8, core: 2. Of those that a mesh axis runs over, the one named last changes fastest.
Arguments:
- trial: bfloat16 [2, 256, 256, 256], P(None, 'sec'), may hold values from -16 to 16
- left_env: bfloat16 [32, 256, 256, 256], P('op', 'sec'), may hold values from -2 to 2
- right_env: bfloat16 [32, 256, 256, 256], P('op', 'sec'), may hold values from -2 to 2
- left_block_ham: bfloat16 [256, 256, 256], P('sec', 'op'), may hold values from -1 to 3
- right_block_ham: bfloat16 [256, 256, 256], P('sec'), may hold values from -1 to 3
- target: int32 [32, 256], P('op', 'sec'), may hold values from 0 to 255, as said below
Outputs:
- hpsi: bfloat16 [2, 256, 256, 256], P(None, 'sec', 'op')
- gram: float32 [2, 2], replicated
The draws below stay inside these ranges and needn't reach their ends.
Inputs may be any that keep to these rules, and one draw needn't show every extreme that they name: Within one device's block of target (4 terms by 8 sectors) at most 2 entries name sectors of any one owner (owner of sector t is t // 8), and some owner is named exactly 2 times.
All inputs are finite; a program needn't handle non-finite values.
Results may differ from the reference program's by a relative error of at most 0.0055.
Values may be sent and summed in bfloat16 or wider, within the bound.
No kernel may reach another device: no remote copies, remote signals or barrier semaphores. Data moves between devices by JAX's collectives and lax.ppermute only.
A program may use at most 128 MiB of HBM per device.

```python
import jax
import jax.numpy as jnp
from jax import lax

BLK = 256
TERMS_DEV = 4
SEC_DEV = 8
TERMS = 32
SECTORS = 256
CAP = 2
N_SEC = 32
N_OP = 8


def with_identity(noise, diagonal_values):
    index = jnp.arange(BLK)
    eye = (index[:, None] == index[None, :]).astype(jnp.float32)
    return eye * diagonal_values + noise


def draw_trial(key, part):
    key = jax.random.fold_in(key, 5)
    first, second, third = jax.random.split(key, 3)
    ramp = 0.5 * 3.0 ** (jnp.arange(SECTORS, dtype=jnp.float32) / (SECTORS - 1))
    ramp = ramp[None, :, None, None]
    signs = jnp.where(jax.random.bernoulli(third, 0.5, (2, SECTORS, 1, 1)), 1.0, -1.0)
    shape = (2, SECTORS, BLK, BLK)
    values = jnp.clip(jax.random.normal(first, shape, jnp.float32), -5.0, 5.0)
    common = jnp.clip(jax.random.normal(second, (2, 1, BLK, BLK), jnp.float32), -5.0, 5.0)
    mixed = 0.8 * signs * common + 0.6 * values
    return (mixed * ramp).astype(jnp.bfloat16)


def environment(key):
    first, second = jax.random.split(key)
    shape = (TERMS, SECTORS, BLK, BLK)
    noise = jnp.clip(jax.random.normal(first, shape, jnp.float32), -4.0, 4.0)
    gains = jax.random.uniform(second, (TERMS, SECTORS, 1, 1), jnp.float32, 0.5, 1.3)
    values = with_identity(0.6 * noise / jnp.sqrt(BLK * 1.0), jnp.ones((BLK,), jnp.float32))
    return (values * gains * TERMS_DEV ** (-0.25)).astype(jnp.bfloat16)


def draw_left_env(key, part):
    key = jax.random.fold_in(key, 1)
    return environment(key)


def draw_right_env(key, part):
    key = jax.random.fold_in(key, 2)
    return environment(key)


def block_ham(key):
    first, second = jax.random.split(key)
    shape = (SECTORS, BLK, BLK)
    noise = jnp.clip(jax.random.normal(first, shape, jnp.float32), -4.0, 4.0)
    levels = jnp.exp(jax.random.uniform(second, (SECTORS, 1, BLK), jnp.float32, jnp.log(0.25), jnp.log(1.0)))
    return with_identity(0.25 * noise / jnp.sqrt(BLK * 1.0), levels).astype(jnp.bfloat16)


def draw_left_block_ham(key, part):
    key = jax.random.fold_in(key, 3)
    return block_ham(key)


def draw_right_block_ham(key, part):
    key = jax.random.fold_in(key, 4)
    return block_ham(key)


def draw_target(key, part):
    key = jax.random.fold_in(key, 11)
    live = TERMS_DEV * SEC_DEV
    slots = N_SEC * CAP

    def one_block(block_key):
        first, second, third, fourth = jax.random.split(block_key, 4)
        owners = jax.random.permutation(first, N_SEC)
        others = CAP + jax.random.permutation(second, slots - CAP)
        chosen = jnp.concatenate([jnp.arange(CAP), others[:live - CAP]])
        chosen = jax.random.permutation(third, chosen)
        owner = owners[chosen // CAP]
        within = jax.random.randint(fourth, (live,), 0, SEC_DEV)
        return (owner * SEC_DEV + within).reshape(TERMS_DEV, SEC_DEV)
    blocks = jax.vmap(one_block)(jax.random.split(key, N_OP * N_SEC))
    blocks = blocks.reshape(N_OP, N_SEC, TERMS_DEV, SEC_DEV).transpose(0, 2, 1, 3)
    return blocks.reshape(TERMS, SECTORS).astype(jnp.int32)


def setup_inputs(seed: int = 0) -> dict:
    key_list = jax.random.split(jax.random.key(seed), 7)
    return {
        "trial": draw_trial(jax.random.fold_in(key_list[6], 71), 0),
        "left_env": draw_left_env(jax.random.fold_in(key_list[6], 71), 0),
        "right_env": draw_right_env(jax.random.fold_in(key_list[6], 71), 0),
        "left_block_ham": draw_left_block_ham(jax.random.fold_in(key_list[6], 71), 0),
        "right_block_ham": draw_right_block_ham(jax.random.fold_in(key_list[6], 71), 0),
        "target": draw_target(jax.random.fold_in(key_list[6], 71), 0),
    }


def reference(trial, left_env, right_env, left_block_ham, right_block_ham, target):
    trial_wide = trial.astype(jnp.float32)

    def one_term(carried, inputs):
        left_term, right_term, term_target = inputs
        halfway = jnp.einsum('sij,vsjk->vsik', left_term.astype(jnp.float32), trial_wide).astype(jnp.bfloat16)
        pieces = jnp.einsum('vsik,skl->vsil', halfway.astype(jnp.float32), right_term.astype(jnp.float32)).astype(jnp.bfloat16)
        carried = carried.at[:, term_target].add(pieces.astype(jnp.float32))
        return carried, None

    start = jnp.zeros((2, SECTORS, BLK, BLK), jnp.float32)
    carried, unused = lax.scan(one_term, start, (left_env, right_env, target.astype(jnp.int32)))
    local = jnp.einsum('sij,vsjk->vsik', left_block_ham.astype(jnp.float32), trial_wide)
    local = local + jnp.einsum('vsij,sjk->vsik', trial_wide, right_block_ham.astype(jnp.float32))
    total = carried + local
    gram = jnp.einsum('asij,bsij->ab', trial_wide, total) / (SECTORS * BLK * BLK)
    return total.astype(jnp.bfloat16), gram
```

```python
import functools

import jax
import jax.numpy as jnp
from jax import lax
from jax.experimental import pallas as pl
from jax.experimental.pallas import tpu as pltpu
from jax.sharding import Mesh
from jax.sharding import PartitionSpec as P

BF16 = jnp.bfloat16
F32 = jnp.float32


def contract_kernel(groups, rows, left_ref, right_ref, trial_ref, out_ref):
    for s in range(left_ref.shape[1]):
        half = jnp.dot(left_ref[0, s], trial_ref[0, s], preferred_element_type=F32).astype(BF16)
        piece = jnp.dot(half, right_ref[0, s], preferred_element_type=F32).astype(BF16)
        width = out_ref.shape[-1]
        for j in range(out_ref.shape[0]):
            out_ref[j, :, s] = piece[:, j * width : (j + 1) * width].reshape(groups, rows, width)


def contract(trial, left_env, right_env, v, groups, parts):
    terms, sectors, size, _ = left_env.shape
    rows = size // groups
    width = size // parts
    return pl.pallas_call(
        functools.partial(contract_kernel, groups, rows),
        grid=(terms,),
        in_specs=[
            pl.BlockSpec((1, sectors, size, size), lambda w: (w, 0, 0, 0)),
            pl.BlockSpec((1, sectors, size, size), lambda w: (w, 0, 0, 0)),
            pl.BlockSpec((1, sectors, size, size), lambda w: (v, 0, 0, 0)),
        ],
        out_specs=pl.BlockSpec((parts, groups, sectors, rows, width), lambda w: (0, 0, w, 0, 0)),
        out_shape=jax.ShapeDtypeStruct((parts, groups, terms * sectors, rows, width), BF16),
        cost_estimate=pl.CostEstimate(
            flops=4 * terms * sectors * size**3,
            bytes_accessed=6 * terms * sectors * size * size,
            transcendentals=0,
        ),
        compiler_params=pltpu.CompilerParams(vmem_limit_bytes=32 * 2**20),
    )(left_env, right_env, trial)


def merge_kernel(target_ref, pieces_ref, out_ref, sums):
    sums[...] = jnp.zeros_like(sums)

    def add(p, carry):
        t = target_ref[p]
        sums[t] += pieces_ref[p].astype(F32)
        return carry

    lax.fori_loop(0, pieces_ref.shape[0], add, 0, unroll=8)
    out_ref[...] = sums[...].astype(BF16)


def merge(targets, pieces, sectors):
    count, rows, width = pieces.shape
    return pl.pallas_call(
        merge_kernel,
        in_specs=[
            pl.BlockSpec(memory_space=pltpu.SMEM),
            pl.BlockSpec(memory_space=pltpu.VMEM),
        ],
        out_specs=pl.BlockSpec(memory_space=pltpu.VMEM),
        out_shape=jax.ShapeDtypeStruct((sectors, rows, width), BF16),
        scratch_shapes=[pltpu.VMEM((sectors, rows, width), F32)],
        cost_estimate=pl.CostEstimate(
            flops=count * rows * width,
            bytes_accessed=2 * (count + sectors) * rows * width,
            transcendentals=0,
        ),
        compiler_params=pltpu.CompilerParams(vmem_limit_bytes=32 * 2**20),
    )(targets, pieces)


PARTS = 2


def body(trial, left_env, right_env, left_block_ham, right_block_ham, target):
    nz, nx = lax.axis_size("z"), lax.axis_size("x")
    groups = lax.axis_size("y") * lax.axis_size("core")
    op = ("y", "core")
    terms, here, size, _ = left_env.shape
    pairs = terms * here
    sectors = nz * nx * here
    rows = size // groups
    width = size // PARTS
    all_targets = lax.all_to_all(
        jnp.broadcast_to(target.reshape(1, pairs), (groups, pairs)), op, 0, 0, tiled=True
    ).reshape(groups * pairs)

    first_row = lax.axis_index(op) * rows
    trial_rows = lax.dynamic_slice_in_dim(trial, first_row, rows, 2)
    local = jnp.einsum("sij,vsjk->vsik", left_block_ham, trial, preferred_element_type=F32)
    local = local + jnp.einsum(
        "vsij,sjk->vsik", trial_rows, right_block_ham, preferred_element_type=F32
    )

    carried = []
    for v in range(trial.shape[0]):
        pieces = contract(trial, left_env, right_env, v, groups, PARTS)
        sums = []
        for j in range(PARTS):
            got = lax.all_to_all(pieces[j], op, 0, 0, tiled=True)
            dense = merge(all_targets, got.reshape(groups * pairs, rows, width), sectors)
            part = lax.psum_scatter(dense, "z", scatter_dimension=0, tiled=True)
            part = lax.all_to_all(part.reshape(nx, here, rows, width), "x", 0, 0, tiled=True)
            sums.append(jnp.sum(part.astype(F32), axis=0))
        carried.append(jnp.concatenate(sums, axis=-1))
    total = jnp.stack(carried) + local
    scale = 1.0 / (sectors * size * size)
    partial = jnp.einsum("asij,bsij->ab", trial_rows.astype(F32), total) * scale

    def spread(x, axes, n):
        x = lax.all_to_all(jnp.broadcast_to(x[None], (n, *x.shape)), axes, 0, 0, tiled=True)
        return jnp.sum(x, axis=0)

    gram = spread(spread(partial, ("z", "x"), nz * nx), op, groups)
    return total.astype(BF16), gram


def solution(mesh):
    sizes = {"z": 8, "x": 4, "y": 4, "core": 2}
    fine = Mesh(mesh.devices.reshape(tuple(sizes.values())), tuple(sizes))
    sec, op = ("z", "x"), ("y", "core")
    return jax.shard_map(
        body,
        mesh=fine,
        in_specs=(
            P(None, sec, None, None),
            P(op, sec, None, None),
            P(op, sec, None, None),
            P(sec, op, None),
            P(sec, None, None),
            P(op, sec),
        ),
        out_specs=(P(None, sec, op, None), P()),
        check_vma=False,
    )
```

```python
import jax
import jax.numpy as jnp
from jax import lax
from jax.experimental import pallas as pl
from jax.experimental.pallas import tpu as pltpu
from jax.sharding import Mesh
from jax.sharding import PartitionSpec as P

BF16 = jnp.bfloat16
F32 = jnp.float32
SUB, LANES = 16, 128


def params(mib):
    return pltpu.CompilerParams(vmem_limit_bytes=mib * 2**20)


def contract_kernel(left_ref, right_ref, trial_ref, out_ref):
    groups = 8
    for s in range(left_ref.shape[1]):
        for v in range(2):
            half = jnp.dot(left_ref[0, s], trial_ref[v, s], preferred_element_type=F32)
            piece = jnp.dot(half.astype(BF16), right_ref[0, s], preferred_element_type=F32)
            piece = piece.astype(BF16)
            for j in range(2):
                cols = piece[:, j * LANES : (j + 1) * LANES].reshape(groups, 2, SUB, LANES)
                for i in range(2):
                    x = 2 * i + j
                    out_ref[x * groups : (x + 1) * groups, s, v] = cols[:, i]


def contract(trial, left_env, right_env, devices):
    terms, here, size, _ = left_env.shape
    cut = 1
    some = here // cut
    return pl.pallas_call(
        contract_kernel,
        grid=(cut, terms),
        in_specs=[
            pl.BlockSpec((1, some, size, size), lambda h, w: (w, h, 0, 0)),
            pl.BlockSpec((1, some, size, size), lambda h, w: (w, h, 0, 0)),
            pl.BlockSpec((2, some, size, size), lambda h, w: (0, h, 0, 0)),
        ],
        out_specs=pl.BlockSpec(
            (devices, some, 2, SUB, LANES), lambda h, w: (0, w * cut + h, 0, 0, 0)
        ),
        out_shape=jax.ShapeDtypeStruct((devices, terms * here, 2, SUB, LANES), BF16),
        cost_estimate=pl.CostEstimate(
            flops=8 * terms * here * size**3,
            bytes_accessed=8 * terms * here * size * size,
            transcendentals=0,
        ),
        compiler_params=params(40),
    )(left_env, right_env, trial)


def merge_kernel(target_ref, pieces_ref, out_ref, sums):
    step = pl.program_id(0)
    sources, pairs = pieces_ref.shape[:2]

    @pl.when(step == 0)
    def _():
        sums[...] = jnp.zeros_like(sums)

    for a in range(sources):

        def add(p, carry, a=a):
            t = target_ref[(step * sources + a) * pairs + p]
            sums[t] += pieces_ref[a, p].astype(F32)
            return carry

        lax.fori_loop(0, pairs, add, 0, unroll=8)

    @pl.when(step == pl.num_programs(0) - 1)
    def _():
        out_ref[...] = sums[...].astype(BF16)


def merge(targets, pieces, sectors):
    devices, pairs = pieces.shape[:2]
    steps = 8
    return pl.pallas_call(
        merge_kernel,
        grid=(steps,),
        in_specs=[
            pl.BlockSpec(memory_space=pltpu.SMEM),
            pl.BlockSpec((devices // steps, pairs, 2, SUB, LANES), lambda i: (i, 0, 0, 0, 0)),
        ],
        out_specs=pl.BlockSpec((sectors, 2, SUB, LANES), lambda i: (0, 0, 0, 0)),
        out_shape=jax.ShapeDtypeStruct((sectors, 2, SUB, LANES), BF16),
        scratch_shapes=[pltpu.VMEM((sectors, 2, SUB, LANES), F32)],
        cost_estimate=pl.CostEstimate(
            flops=devices * pairs * 2 * SUB * LANES,
            bytes_accessed=2 * (devices * pairs + sectors) * 2 * SUB * LANES,
            transcendentals=0,
        ),
        compiler_params=params(32),
    )(targets, pieces)


def finish_kernel(scale, got_ref, local_ref, rows_ref, out_ref, gram_ref):
    nz = got_ref.shape[0]
    found = [[jnp.zeros((SUB, LANES), F32) for _ in range(2)] for _ in range(2)]
    for x in range(4):
        i, j = x // 2, x % 2
        acc = got_ref[0, x].astype(F32)
        for z in range(1, nz):
            acc = acc + got_ref[z, x].astype(F32)
        here = (slice(None), slice(i * SUB, (i + 1) * SUB), slice(j * LANES, (j + 1) * LANES))
        for b in range(2):
            total = acc[:, b] + local_ref[(b, *here)]
            out_ref[(b, *here)] = total.astype(BF16)
            for a in range(2):
                found[a][b] += jnp.sum(rows_ref[(a, *here)].astype(F32) * total, axis=0)
    for a in range(2):
        for b in range(2):
            gram_ref[a, b] = jnp.sum(found[a][b]) * scale


def finish(got, local, trial_rows, scale):
    vmem = pl.BlockSpec(memory_space=pltpu.VMEM)
    return pl.pallas_call(
        lambda *refs: finish_kernel(scale, *refs),
        in_specs=[vmem] * 3,
        out_specs=[vmem, pl.BlockSpec(memory_space=pltpu.SMEM)],
        out_shape=[
            jax.ShapeDtypeStruct(local.shape, BF16),
            jax.ShapeDtypeStruct((2, 2), F32),
        ],
        compiler_params=params(32),
    )(got, local, trial_rows)


def to_all(x, axes):
    return lax.all_to_all(x, axes, 0, 0, tiled=True)


def spread(x, axes):
    return to_all(jnp.broadcast_to(x[None], (lax.axis_size(axes), *x.shape)), axes)


def body(trial, left_env, right_env, left_block_ham, right_block_ham, target):
    sec, op, plane = ("z", "x"), ("y", "core"), ("x", "y", "core")
    nz, nx, devices = lax.axis_size("z"), lax.axis_size("x"), lax.axis_size(plane)
    terms, here, size, _ = left_env.shape
    sectors = nz * nx * here
    rows = size // lax.axis_size(op)
    targets = spread(target.reshape(terms * here), plane).reshape(-1)

    first_row = lax.axis_index(op) * rows
    trial_rows = lax.dynamic_slice_in_dim(trial, first_row, rows, 2)
    local = jnp.einsum("sij,vsjk->vsik", left_block_ham, trial, preferred_element_type=F32)
    local = local + jnp.einsum(
        "vsij,sjk->vsik", trial_rows, right_block_ham, preferred_element_type=F32
    )

    pieces = to_all(contract(trial, left_env, right_env, devices), plane)
    sums = to_all(merge(targets, pieces, sectors).reshape(-1, here, 2, SUB, LANES), sec)
    scale = 1.0 / (sectors * size * size)
    hpsi, partial = finish(sums.reshape(nz, nx, here, 2, SUB, LANES), local, trial_rows, scale)
    gram = jnp.sum(spread(partial, sec), axis=0)
    gram = jnp.sum(spread(gram, op), axis=0)
    return hpsi, gram


def solution(mesh):
    sizes = {"z": 8, "x": 4, "y": 4, "core": 2}
    fine = Mesh(mesh.devices.reshape(tuple(sizes.values())), tuple(sizes))
    sec, op = ("z", "x"), ("y", "core")
    return jax.shard_map(
        body,
        mesh=fine,
        in_specs=(
            P(None, sec, None, None),
            P(op, sec, None, None),
            P(op, sec, None, None),
            P(sec, op, None),
            P(sec, None, None),
            P(op, sec),
        ),
        out_specs=(P(None, sec, op, None), P()),
        check_vma=False,
    )
```

```python
import functools

import jax
import jax.numpy as jnp
from jax import lax
from jax.experimental import pallas as pl
from jax.experimental.pallas import tpu as pltpu
from jax.sharding import Mesh
from jax.sharding import PartitionSpec as P

BF16 = jnp.bfloat16
F32 = jnp.float32
RING = 4
GROUPS = 8
SUB = 16
VMEM = pl.BlockSpec(memory_space=pltpu.VMEM)
SMEM = pl.BlockSpec(memory_space=pltpu.SMEM)
ANY = pl.BlockSpec(memory_space=pl.ANY)


def params(mib):
    return pltpu.CompilerParams(vmem_limit_bytes=mib * 2**20)


def contract_kernel(part, hint_ref, place_ref, slab_ref, left_ref, right_ref, trial_ref, *outs):
    step = pl.program_id(0)
    here, size = left_ref.shape[1], left_ref.shape[3]
    if part == 1:
        order = [SUB * (2 * r + 1) for r in range(GROUPS)]
    else:
        x, core = place_ref[0], place_ref[1]
        order = [
            pl.multiple_of(((x + k) % RING * 2 + c) * 2 * SUB, SUB)
            for c in (core, 1 - core)
            for k in range(RING)
        ]
    each = GROUPS // len(outs)

    @pl.when(step == 0)
    def _():
        for out in outs:
            for g in range(each):
                for v in range(2):
                    out[g, out.shape[1] - 1, v] = slab_ref[...]

    for s in range(here):
        rows = jnp.concatenate([left_ref[0, s, pl.ds(a, SUB), :] for a in order], axis=0)
        for v in range(2):
            half = jnp.dot(rows, trial_ref[v, s], preferred_element_type=F32).astype(BF16)
            piece = jnp.dot(half, right_ref[0, s], preferred_element_type=F32).astype(BF16)
            piece = piece.reshape(GROUPS, SUB, size)
            for n, out in enumerate(outs):
                out[:, step * here + s, v] = piece[n * each : (n + 1) * each]


def contract(part, hint, place, slab, trial, left_env, right_env):
    terms, here, size, _ = left_env.shape
    outs = (2, 1)[part]
    shape = (GROUPS // outs, terms * here + 1, 2, SUB, size)
    return pl.pallas_call(
        functools.partial(contract_kernel, part),
        grid=(terms,),
        in_specs=[
            ANY,
            SMEM,
            VMEM,
            pl.BlockSpec((1, here, size, size), lambda w: (w, 0, 0, 0)),
            pl.BlockSpec((1, here, size, size), lambda w: (w, 0, 0, 0)),
            pl.BlockSpec((2, here, size, size), lambda w: (0, 0, 0, 0)),
        ],
        out_specs=[pl.BlockSpec(shape, lambda w: (0, 0, 0, 0, 0))] * outs,
        out_shape=[jax.ShapeDtypeStruct(shape, BF16)] * outs,
        cost_estimate=pl.CostEstimate(
            flops=4 * terms * here * size**3,
            bytes_accessed=8 * terms * here * size * size,
            transcendentals=0,
        ),
        compiler_params=params(56),
    )(hint, place, slab, left_env, right_env, trial)


def pack_kernel(mine_ref, got_ref, *outs):
    for k in range(RING):
        outs[k][0] = mine_ref[k]
        outs[k][1] = got_ref[k]


def pack(mine, got):
    shape = jax.ShapeDtypeStruct((2, *mine.shape[1:]), BF16)
    return pl.pallas_call(
        pack_kernel,
        in_specs=[VMEM] * 2,
        out_specs=[VMEM] * RING,
        out_shape=[shape] * RING,
        cost_estimate=pl.CostEstimate(
            flops=0, bytes_accessed=14 * mine.size // 4, transcendentals=0
        ),
        compiler_params=params(60),
    )(mine, got)


def merge_kernel(z_first, hint_ref, *refs):
    ins, out = refs[:-4], refs[-4]
    rows, table, sums = refs[-3:]
    sources = [(ref, j) for ref in ins for j in range(ref.shape[0])]
    pairs = ins[0].shape[1] - 1

    def fetch(sem):
        for i, (ref, j) in enumerate(sources):
            rows[i : i + 1, :] = ref[j, pairs, 0, :, :128].astype(F32)[0:1].astype(jnp.int32)
        copy = pltpu.make_async_copy(rows, table, sem)
        copy.start()
        sums[...] = jnp.zeros_like(sums)
        copy.wait()

    pl.run_scoped(fetch, pltpu.SemaphoreType.DMA)
    for i, (ref, j) in enumerate(sources):

        def add(p, carry, i=i, ref=ref, j=j):
            t = table[i, p]
            slot = t if z_first else t // 8 % RING * 64 + t // 32 * 8 + t % 8
            sums[slot] += ref[j, p].astype(F32)
            return carry

        lax.fori_loop(0, pairs, add, 0, unroll=8)
    out[...] = sums[...].astype(BF16)


def merge(hint, blocks, sectors, z_first):
    block = blocks[0].shape[2:]
    return pl.pallas_call(
        functools.partial(merge_kernel, z_first),
        in_specs=[ANY] + [VMEM] * len(blocks),
        out_specs=VMEM,
        out_shape=jax.ShapeDtypeStruct((sectors, *block), BF16),
        scratch_shapes=[
            pltpu.VMEM((GROUPS, 128), jnp.int32),
            pltpu.SMEM((GROUPS, 128), jnp.int32),
            pltpu.VMEM((sectors, *block), F32),
        ],
        cost_estimate=pl.CostEstimate(flops=2**22, bytes_accessed=2**23, transcendentals=0),
        compiler_params=params(40),
    )(hint, *blocks)


def reduce_kernel(blocks, out):
    out[...] = sum(blocks[x].astype(F32) for x in range(RING)).astype(BF16)


def reduce(blocks):
    _, count, *rest = blocks.shape
    steps = 8
    return pl.pallas_call(
        reduce_kernel,
        grid=(steps,),
        in_specs=[pl.BlockSpec((RING, count // steps, *rest), lambda i: (0, i, 0, 0, 0))],
        out_specs=pl.BlockSpec((count // steps, *rest), lambda i: (i, 0, 0, 0)),
        out_shape=jax.ShapeDtypeStruct((count, *rest), BF16),
        cost_estimate=pl.CostEstimate(flops=2**22, bytes_accessed=2**22, transcendentals=0),
        compiler_params=params(24),
    )(blocks)


def finish_kernel(scale, first, second, local, trial_rows, out, gram):
    size = out.shape[-1]
    found = [[jnp.zeros((SUB, size), F32) for _ in range(2)] for _ in range(2)]
    for half in range(2):
        rows = slice(half * SUB, (half + 1) * SUB)
        for b in range(2):
            if half == 0:
                total = first[:, b].astype(F32)
            else:
                total = sum(second[z, :, b].astype(F32) for z in range(second.shape[0]))
            total = total + local[b, :, rows]
            out[b, :, rows] = total.astype(BF16)
            for a in range(2):
                found[a][b] += jnp.sum(trial_rows[a, :, rows].astype(F32) * total, axis=0)
    for a in range(2):
        for b in range(2):
            gram[a, b] = jnp.sum(found[a][b]) * scale


def finish(scale, *args):
    local = args[2]
    return pl.pallas_call(
        functools.partial(finish_kernel, scale),
        in_specs=[VMEM] * 4,
        out_specs=[VMEM, SMEM],
        out_shape=[
            jax.ShapeDtypeStruct(local.shape, BF16),
            jax.ShapeDtypeStruct((2, 2), F32),
        ],
        cost_estimate=pl.CostEstimate(flops=2**21, bytes_accessed=2**21, transcendentals=0),
        compiler_params=params(24),
    )(*args)


def to_all(x, axes):
    return lax.all_to_all(x, axes, 0, 0, tiled=True)


def spread(x, axes):
    return to_all(jnp.broadcast_to(x[None], (lax.axis_size(axes), *x.shape)), axes)


def shift(x, axis, k):
    n = lax.axis_size(axis)
    return lax.ppermute(x, axis, [(i, (i + k) % n) for i in range(n)])


def swap(x):
    return lax.ppermute(x, "core", [(0, 1), (1, 0)])


def turn(x):
    pairs = [(a * RING + b, b * RING + a) for a in range(RING) for b in range(RING)]
    return lax.ppermute(x, ("x", "y"), pairs)


def body(trial, left_env, right_env, left_block_ham, right_block_ham, target):
    op = ("y", "core")
    nz, nx = lax.axis_size("z"), lax.axis_size("x")
    terms, here, size, _ = left_env.shape
    sectors = nz * nx * here
    rows = size // lax.axis_size(op)
    places = [lax.axis_index(name) for name in ("x", "core", "y", "z")]
    place = jnp.stack(places)
    place = place.astype(jnp.int32)
    pairs = terms * here
    slab = jnp.pad(target.reshape(1, pairs).astype(BF16), ((0, SUB - 1), (0, size - pairs)))

    first_row = lax.axis_index(op) * rows
    trial_rows = lax.dynamic_slice_in_dim(trial, first_row, rows, 2)
    local = jnp.einsum("sij,vsjk->vsik", left_block_ham, trial, preferred_element_type=F32)
    local = local + jnp.einsum(
        "vsij,sjk->vsik", trial_rows, right_block_ham, preferred_element_type=F32
    )

    (pieces,) = contract(1, slab, place, slab, trial, left_env, right_env)
    mine, other = contract(0, pieces, place, slab, trial, left_env, right_env)
    pieces = to_all(pieces, op)
    packed = pack(mine, swap(other))
    arrived = [shift(packed[k], "x", k) for k in range(1, RING)]

    blocks = merge(slab, [pieces], sectors, False)
    dense = merge(blocks, [packed[0], *arrived], sectors, True)
    blocks = to_all(blocks.reshape(nx, nz * here, 2, SUB, size), "x")
    reduced = lax.psum_scatter(dense, "z", scatter_dimension=0, tiled=True)
    second = to_all(reduce(blocks).reshape(nz, here, 2, SUB, size), "z")

    reduced = reduced.reshape(nx, here, 2, SUB, size)
    y = places[2]
    first = lax.dynamic_index_in_dim(reduced, y, 0, keepdims=False).astype(F32)
    for k in range(1, RING):
        block = lax.dynamic_index_in_dim(reduced, (y + k) % RING, 0, keepdims=False)
        first = first + shift(block, "y", k).astype(F32)
    first = turn(first.astype(BF16))

    scale = 1.0 / (sectors * size * size)
    hpsi, gram = finish(scale, first, second, local, trial_rows)
    gram = jnp.sum(spread(gram, ("z", "x")), axis=0)
    gram = jnp.sum(spread(gram, op), axis=0)
    return hpsi, gram


def solution(mesh):
    sizes = {"z": 8, "x": 4, "y": 4, "core": 2}
    fine = Mesh(mesh.devices.reshape(tuple(sizes.values())), tuple(sizes))
    sec, op = ("z", "x"), ("y", "core")
    return jax.shard_map(
        body,
        mesh=fine,
        in_specs=(
            P(None, sec, None, None),
            P(op, sec, None, None),
            P(op, sec, None, None),
            P(sec, op, None),
            P(sec, None, None),
            P(op, sec),
        ),
        out_specs=(P(None, sec, op, None), P()),
        check_vma=False,
    )
```

```python
import functools

import jax
import jax.numpy as jnp
from jax import lax
from jax.experimental import pallas as pl
from jax.experimental.pallas import tpu as pltpu
from jax.sharding import Mesh
from jax.sharding import PartitionSpec as P

BF16 = jnp.bfloat16
F32 = jnp.float32
RING = 4
GROUPS = 8
SUB = 16
STEPS = 8
VMEM = pl.BlockSpec(memory_space=pltpu.VMEM)
SMEM = pl.BlockSpec(memory_space=pltpu.SMEM)
HBM = pl.BlockSpec(memory_space=pltpu.HBM)


def params(mib):
    return pltpu.CompilerParams(vmem_limit_bytes=mib * 2**20)


def contract_kernel(target_ref, left_ref, right_ref, trial_ref, *refs):
    outs, (stage, slab, wide, sems, slab_sems) = refs[: 1 + RING], refs[1 + RING :]
    step = pl.program_id(0)
    last = pl.num_programs(0) - 1
    here, size = left_ref.shape[1], left_ref.shape[3]
    x, core = lax.axis_index("x"), lax.axis_index("core")
    order = [SUB * (2 * r + 1) for r in range(GROUPS)]
    order += [
        pl.multiple_of(((x + k) % RING * 2 + c) * 2 * SUB, SUB)
        for k in range(RING)
        for c in (core, 1 - core)
    ]
    places = [(0, GROUPS)] + [(GROUPS + 2 * k, 2) for k in range(RING)]

    def copies(i):
        rows = pl.ds(i * here, here)
        return [
            pltpu.make_async_copy(
                stage.at[i % 2, pl.ds(a, n)], out.at[:, rows], sems.at[i % 2, j]
            )
            for j, (out, (a, n)) in enumerate(zip(outs, places, strict=True))
        ]

    def slab_copies():
        return [
            pltpu.make_async_copy(
                slab.at[pl.ds(0, n)], out.at[:, pl.ds(here * (last + 1), 1)], slab_sems.at[j]
            )
            for j, (out, (_, n)) in enumerate(zip(outs, places, strict=True))
        ]

    @pl.when(step == 0)
    def _():
        wide[...] = jnp.zeros_like(wide)
        wide[:4, :8] = target_ref[...].astype(F32)
        for g in range(GROUPS):
            for v in range(2):
                slab[g, 0, v] = wide[...].astype(BF16)
        for copy in slab_copies():
            copy.start()

    @pl.when(step >= 2)
    def _():
        for copy in copies(step - 2):
            copy.wait()

    for s in range(here):
        rows = jnp.concatenate([left_ref[0, s, pl.ds(a, SUB), :] for a in order], axis=0)
        half = [
            jnp.dot(rows, trial_ref[v, s], preferred_element_type=F32).astype(BF16)
            for v in range(2)
        ]
        half = jnp.concatenate(half, axis=0)
        piece = jnp.dot(half, right_ref[0, s], preferred_element_type=F32).astype(BF16)
        piece = piece.reshape(2, 2 * GROUPS, SUB, size)
        for v in range(2):
            stage[step % 2, :, s, v] = piece[v]
    for copy in copies(step):
        copy.start()

    @pl.when(step == last)
    def _():
        for copy in copies(step - 1) + copies(step) + slab_copies():
            copy.wait()


def contract(target, trial, left_env, right_env):
    terms, here, size, _ = left_env.shape
    shapes = [(n, terms * here + 1, 2, SUB, size) for n in (GROUPS, 2, 2, 2, 2)]
    return pl.pallas_call(
        contract_kernel,
        grid=(terms,),
        in_specs=[
            VMEM,
            pl.BlockSpec((1, here, size, size), lambda w: (w, 0, 0, 0)),
            pl.BlockSpec((1, here, size, size), lambda w: (w, 0, 0, 0)),
            pl.BlockSpec((2, here, size, size), lambda w: (0, 0, 0, 0)),
        ],
        out_specs=[HBM] * len(shapes),
        out_shape=[jax.ShapeDtypeStruct(shape, BF16) for shape in shapes],
        scratch_shapes=[
            pltpu.VMEM((2, 2 * GROUPS, here, 2, SUB, size), BF16),
            pltpu.VMEM((GROUPS, 1, 2, SUB, size), BF16),
            pltpu.VMEM((SUB, size), F32),
            pltpu.SemaphoreType.DMA((2, len(shapes))),
            pltpu.SemaphoreType.DMA((len(shapes),)),
        ],
        cost_estimate=pl.CostEstimate(
            flops=8 * terms * here * size**3,
            bytes_accessed=8 * terms * here * size * size,
            transcendentals=0,
        ),
        compiler_params=params(56),
    )(target, left_env, right_env, trial)


def pack_kernel(*refs):
    ins, out, sems = refs[:RING], refs[-2], refs[-1]
    copies = [
        pltpu.make_async_copy(ref.at[1], out.at[k], sems.at[k]) for k, ref in enumerate(ins)
    ]
    for copy in copies:
        copy.start()
    for copy in copies:
        copy.wait()


def pack(blocks):
    shape = blocks[0].shape[1:]
    return pl.pallas_call(
        pack_kernel,
        in_specs=[HBM] * RING,
        out_specs=HBM,
        out_shape=jax.ShapeDtypeStruct((RING, *shape), BF16),
        scratch_shapes=[pltpu.SemaphoreType.DMA((RING,))],
        cost_estimate=pl.CostEstimate(
            flops=0, bytes_accessed=4 * blocks[0].size, transcendentals=0
        ),
        compiler_params=params(24),
    )(*blocks)


def merge_kernel(z_first, hint_ref, *refs):
    rows, table, sums, stage, table_sem, sems = refs[-6:]
    ins, outs = (refs[: RING + 1], refs[RING + 1 : -6]) if z_first else (refs[:1], refs[1:-6])
    sources = [(ref, j) for ref in ins for j in range(ref.shape[0])]
    pairs = ins[0].shape[1] - 1
    for i, (ref, j) in enumerate(sources):
        line = ref[j, pairs, 0, :, :128].astype(F32)[:8]
        rows[8 * i : 8 * i + 8, :] = line.astype(jnp.int32)
    copy = pltpu.make_async_copy(rows, table, table_sem)
    copy.start()
    sums[...] = jnp.zeros_like(sums)
    copy.wait()
    here = lax.axis_index("z")
    for i, (ref, j) in enumerate(sources):

        def add_line(w, carry, i=i, ref=ref, j=j):
            for s in range(8):
                t = table[8 * i + w, s]
                if z_first:
                    slot = (t // 32 - here) % 8 * 32 + t % 32
                else:
                    slot = t // 8 % RING * 64 + t // 32 * 8 + t % 8
                sums[slot] += ref[j, w * 8 + s].astype(F32)
            return carry

        lax.fori_loop(0, pairs // 8, add_line, 0)
    some = sums.shape[0] // STEPS
    copies = []
    for n in range(STEPS):
        part = pl.ds(n * some, some)
        stage[part] = sums[part].astype(BF16)
        if not z_first:
            pieces = [(part, outs[0].at[part])]
        elif n == 4:
            pieces = [(pl.ds((8 + m) * some // 2, some // 2), outs[1 + m]) for m in range(2)]
        else:
            pieces = [(part, outs[0].at[n])]
        for source, out in pieces:
            copies.append(pltpu.make_async_copy(stage.at[source], out, sems.at[len(copies)]))
            copies[-1].start()
    for copy in copies:
        copy.wait()


def merge(hint, blocks, sectors, z_first):
    block = blocks[0].shape[2:]
    shapes = [(8, 32), (16,), (16,)] if z_first else [(sectors,)]
    full = pl.BlockSpec(blocks[-1].shape, lambda i: (0, 0, 0, 0, 0))
    own = pl.BlockSpec((1, *blocks[-1].shape[1:]), lambda i: (0, 0, 0, 0, 0))
    return pl.pallas_call(
        functools.partial(merge_kernel, z_first),
        grid=(1,),
        in_specs=[HBM] + [own] * (len(blocks) - 1) + [full],
        out_specs=[HBM] * len(shapes),
        out_shape=[jax.ShapeDtypeStruct((*shape, *block), BF16) for shape in shapes],
        scratch_shapes=[
            pltpu.VMEM((GROUPS * 8, 128), jnp.int32),
            pltpu.SMEM((GROUPS * 8, 128), jnp.int32),
            pltpu.VMEM((sectors, *block), F32),
            pltpu.VMEM((sectors, *block), BF16),
            pltpu.SemaphoreType.DMA,
            pltpu.SemaphoreType.DMA((STEPS + 1,)),
        ],
        cost_estimate=pl.CostEstimate(flops=2**22, bytes_accessed=2**23, transcendentals=0),
        compiler_params=params(56),
    )(hint, *blocks)


def join_kernel(first, up_base, down_base, up, down, up_out, down_out):
    half = up.shape[0]
    if first:
        up_out[:half] = (up_base[0, :half].astype(F32) + up[...].astype(F32)).astype(BF16)
        up_out[half:] = up_base[0, half:]
        down_out[:half] = down_base[0, :half]
        down_out[half:] = (down_base[0, half:].astype(F32) + down[...].astype(F32)).astype(BF16)
    else:
        up_out[...] = (up_base[0].astype(F32) + up[...].astype(F32)).astype(BF16)
        down_out[...] = (down_base[0].astype(F32) + down[...].astype(F32)).astype(BF16)


def join(dense, near, up, down):
    shape = dense.shape[1:]
    first = up.shape[0] != shape[0]

    def pick(n):
        return pl.BlockSpec((1, *shape), lambda i: (n, 0, 0, 0, 0))

    return pl.pallas_call(
        functools.partial(join_kernel, first),
        grid=(1,),
        in_specs=[pick(near), pick(8 - near), VMEM, VMEM],
        out_specs=[VMEM] * 2,
        out_shape=[jax.ShapeDtypeStruct(shape, BF16)] * 2,
        cost_estimate=pl.CostEstimate(flops=2**20, bytes_accessed=2**21, transcendentals=0),
        compiler_params=params(56),
    )(dense, dense, up, down)


def settle_kernel(own, up, down, *parts):
    here = parts[0].shape[0]
    y = lax.axis_index("y")
    for k in range(RING):
        rows = pl.ds(pl.multiple_of((y + k) % RING * here, here), here)
        total = own[0, rows].astype(F32) + up[rows].astype(F32) + down[rows].astype(F32)
        parts[k][...] = total.astype(BF16)


def settle(dense, up, down):
    count, *rest = dense.shape[1:]
    return pl.pallas_call(
        settle_kernel,
        grid=(1,),
        in_specs=[pl.BlockSpec((1, count, *rest), lambda i: (0, 0, 0, 0, 0)), VMEM, VMEM],
        out_specs=[VMEM] * RING,
        out_shape=[jax.ShapeDtypeStruct((count // RING, *rest), BF16)] * RING,
        cost_estimate=pl.CostEstimate(flops=2**20, bytes_accessed=2**21, transcendentals=0),
        compiler_params=params(56),
    )(dense, up, down)


def reduce_kernel(blocks, out):
    out[...] = sum(blocks[x].astype(F32) for x in range(RING)).astype(BF16)


def reduce(blocks):
    _, count, *rest = blocks.shape
    steps = 4
    return pl.pallas_call(
        reduce_kernel,
        grid=(steps,),
        in_specs=[pl.BlockSpec((RING, count // steps, *rest), lambda i: (0, i, 0, 0, 0))],
        out_specs=pl.BlockSpec((count // steps, *rest), lambda i: (i, 0, 0, 0)),
        out_shape=jax.ShapeDtypeStruct((count, *rest), BF16),
        cost_estimate=pl.CostEstimate(flops=2**22, bytes_accessed=2**22, transcendentals=0),
        compiler_params=params(56),
    )(blocks)


def gate(x, *waits):
    return pl.pallas_call(
        lambda *refs: None,
        in_specs=[HBM] * (1 + len(waits)),
        out_specs=HBM,
        out_shape=jax.ShapeDtypeStruct(x.shape, x.dtype),
        input_output_aliases={0: 0},
        compiler_params=params(16),
    )(x, *waits)


def finish_kernel(scale, first, second, local, trial_rows, out, gram):
    size = out.shape[-1]
    found = [[jnp.zeros((SUB, size), F32) for _ in range(2)] for _ in range(2)]
    for half in range(2):
        rows = slice(half * SUB, (half + 1) * SUB)
        for b in range(2):
            if half == 0:
                total = first[:, b].astype(F32)
            else:
                total = sum(second[z, :, b].astype(F32) for z in range(second.shape[0]))
            total = total + local[b, :, rows]
            out[b, :, rows] = total.astype(BF16)
            for a in range(2):
                found[a][b] += jnp.sum(trial_rows[a, :, rows].astype(F32) * total, axis=0)
    for a in range(2):
        for b in range(2):
            gram[a, b] = jnp.sum(found[a][b]) * scale


def finish(scale, *args):
    local = args[2]
    return pl.pallas_call(
        functools.partial(finish_kernel, scale),
        in_specs=[VMEM] * 4,
        out_specs=[VMEM, SMEM],
        out_shape=[
            jax.ShapeDtypeStruct(local.shape, BF16),
            jax.ShapeDtypeStruct((2, 2), F32),
        ],
        cost_estimate=pl.CostEstimate(flops=2**21, bytes_accessed=2**21, transcendentals=0),
        compiler_params=params(24),
    )(*args)


def to_all(x, axes):
    return lax.all_to_all(x, axes, 0, 0, tiled=True)


def spread(x, axes):
    return to_all(jnp.broadcast_to(x[None], (lax.axis_size(axes), *x.shape)), axes)


def shift(x, axis, k):
    n = lax.axis_size(axis)
    return lax.ppermute(x, axis, [(i, (i + k) % n) for i in range(n)])


def swap(x):
    return lax.ppermute(x, "core", [(0, 1), (1, 0)])


def turn(x, k):
    pairs = [
        (a * RING + b, (b + k) % RING * RING + a) for a in range(RING) for b in range(RING)
    ]
    return lax.ppermute(x, ("x", "y"), pairs)


def add(*arrays):
    return sum(x.astype(F32) for x in arrays).astype(BF16)


def body(trial, left_env, right_env, left_block_ham, right_block_ham, target):
    op = ("y", "core")
    nz, nx = lax.axis_size("z"), lax.axis_size("x")
    terms, here, size, _ = left_env.shape
    sectors = nz * nx * here
    rows = size // lax.axis_size(op)
    first_row = lax.axis_index(op) * rows
    trial_rows = lax.dynamic_slice_in_dim(trial, first_row, rows, 2)
    local = jnp.einsum("sij,vsjk->vsik", left_block_ham, trial, preferred_element_type=F32)
    local = local + jnp.einsum(
        "vsij,sjk->vsik", trial_rows, right_block_ham, preferred_element_type=F32
    )

    pieces, *strips = contract(target, trial, left_env, right_env)
    pieces = to_all(pieces, op)
    strips = [strips[0]] + [shift(strips[k], "x", k) for k in range(1, RING)]
    others = pack(strips)

    (blocks,) = merge(others, [pieces], sectors, False)
    dense, up, down = merge(blocks, [*strips, swap(others)], sectors, True)
    blocks = to_all(blocks.reshape(nx, nz * here, 2, SUB, size), "x")
    for near in (3, 2, 1):
        up, down = join(dense, near, shift(up, "z", 1), shift(down, "z", -1))
    up, down = shift(up, "z", 1), shift(down, "z", -1)
    halves = gate(reduce(blocks), up, down)
    second = to_all(halves.reshape(nz, here, 2, SUB, size), "z")
    parts = settle(dense, up, down)

    first = add(*(turn(parts[k], k) for k in range(RING)))

    scale = 1.0 / (sectors * size * size)
    hpsi, gram = finish(scale, first, second, local, trial_rows)
    gram = jnp.sum(spread(gram, ("z", "x")), axis=0)
    gram = jnp.sum(spread(gram, op), axis=0)
    return hpsi, gram


def solution(mesh):
    sizes = {"z": 8, "x": 4, "y": 4, "core": 2}
    fine = Mesh(mesh.devices.reshape(tuple(sizes.values())), tuple(sizes))
    sec, op = ("z", "x"), ("y", "core")
    return jax.shard_map(
        body,
        mesh=fine,
        in_specs=(
            P(None, sec, None, None),
            P(op, sec, None, None),
            P(op, sec, None, None),
            P(sec, op, None),
            P(sec, None, None),
            P(op, sec),
        ),
        out_specs=(P(None, sec, op, None), P()),
        check_vma=False,
    )
```

```python
import functools

import jax
import jax.numpy as jnp
from jax import lax
from jax.experimental import pallas as pl
from jax.experimental.pallas import tpu as pltpu
from jax.sharding import Mesh
from jax.sharding import PartitionSpec as P

BF16 = jnp.bfloat16
F32 = jnp.float32
RING = 4
GROUPS = 8
SUB = 16
STEPS = 8
VMEM = pl.BlockSpec(memory_space=pltpu.VMEM)
SMEM = pl.BlockSpec(memory_space=pltpu.SMEM)
HBM = pl.BlockSpec(memory_space=pltpu.HBM)
ANY = pl.BlockSpec(memory_space=pl.ANY)
HINT = jax.ShapeDtypeStruct((8, 128), F32)


def params(mib):
    return pltpu.CompilerParams(vmem_limit_bytes=mib * 2**20)


def contract_kernel(target_ref, left_ref, right_ref, trial_ref, *refs):
    outs, (stage, slab, wide, sems, slab_sems) = refs[: 2 + RING], refs[2 + RING :]
    step = pl.program_id(0)
    last = pl.num_programs(0) - 1
    here, size = left_ref.shape[1], left_ref.shape[3]
    x, core = lax.axis_index("x"), lax.axis_index("core")
    order = [SUB * (2 * r + 1) for r in range(GROUPS)]
    order += [
        pl.multiple_of(((x + k) % RING * 2 + c) * 2 * SUB, SUB)
        for k in range(RING)
        for c in (core, 1 - core)
    ]
    places = [(0, GROUPS), (GROUPS, 1), (GROUPS + 1, 1)]
    places += [(GROUPS + 2 * k, 2) for k in range(1, RING)]

    def copies(i):
        rows = pl.ds(i * here, here)
        return [
            pltpu.make_async_copy(
                stage.at[i % 2, pl.ds(a, n)], out.at[:, rows], sems.at[i % 2, j]
            )
            for j, (out, (a, n)) in enumerate(zip(outs, places, strict=True))
        ]

    def slab_copies():
        return [
            pltpu.make_async_copy(
                slab.at[pl.ds(0, n)], out.at[:, pl.ds(here * (last + 1), 1)], slab_sems.at[j]
            )
            for j, (out, (_, n)) in enumerate(zip(outs, places, strict=True))
        ]

    @pl.when(step == 0)
    def _():
        wide[...] = jnp.zeros_like(wide)
        wide[:4, :8] = target_ref[...].astype(F32)
        for g in range(GROUPS):
            for v in range(2):
                slab[g, 0, v] = wide[...].astype(BF16)
        for copy in slab_copies():
            copy.start()

    @pl.when(step >= 2)
    def _():
        for copy in copies(step - 2):
            copy.wait()

    for s in range(here):
        rows = jnp.concatenate([left_ref[0, s, pl.ds(a, SUB), :] for a in order], axis=0)
        half = [
            jnp.dot(rows, trial_ref[v, s], preferred_element_type=F32).astype(BF16)
            for v in range(2)
        ]
        half = jnp.concatenate(half, axis=0)
        piece = jnp.dot(half, right_ref[0, s], preferred_element_type=F32).astype(BF16)
        piece = piece.reshape(2, 2 * GROUPS, SUB, size)
        for v in range(2):
            stage[step % 2, :, s, v] = piece[v]
    for copy in copies(step):
        copy.start()

    @pl.when(step == last)
    def _():
        for copy in copies(step - 1) + copies(step) + slab_copies():
            copy.wait()


def contract(target, trial, left_env, right_env):
    terms, here, size, _ = left_env.shape
    shapes = [(n, terms * here + 1, 2, SUB, size) for n in (GROUPS, 1, 1, 2, 2, 2)]
    return pl.pallas_call(
        contract_kernel,
        grid=(terms,),
        in_specs=[
            VMEM,
            pl.BlockSpec((1, here, size, size), lambda w: (w, 0, 0, 0)),
            pl.BlockSpec((1, here, size, size), lambda w: (w, 0, 0, 0)),
            pl.BlockSpec((2, here, size, size), lambda w: (0, 0, 0, 0)),
        ],
        out_specs=[HBM] * len(shapes),
        out_shape=[jax.ShapeDtypeStruct(shape, BF16) for shape in shapes],
        scratch_shapes=[
            pltpu.VMEM((2, 2 * GROUPS, here, 2, SUB, size), BF16),
            pltpu.VMEM((GROUPS, 1, 2, SUB, size), BF16),
            pltpu.VMEM((SUB, size), F32),
            pltpu.SemaphoreType.DMA((2, len(shapes))),
            pltpu.SemaphoreType.DMA((len(shapes),)),
        ],
        cost_estimate=pl.CostEstimate(
            flops=8 * terms * here * size**3,
            bytes_accessed=8 * terms * here * size * size,
            transcendentals=0,
        ),
        compiler_params=params(56),
    )(target, left_env, right_env, trial)


def pack_kernel(*refs):
    ins, (out, hint, sems) = refs[: RING - 1], refs[RING - 1 :]
    hint[...] = jnp.zeros_like(hint)
    copies = [
        pltpu.make_async_copy(ref.at[1], out.at[k], sems.at[k]) for k, ref in enumerate(ins)
    ]
    for copy in copies:
        copy.start()
    for copy in copies:
        copy.wait()


def pack(blocks):
    shape = blocks[0].shape[1:]
    return pl.pallas_call(
        pack_kernel,
        in_specs=[HBM] * (RING - 1),
        out_specs=[HBM, VMEM],
        out_shape=[jax.ShapeDtypeStruct((RING - 1, *shape), BF16), HINT],
        scratch_shapes=[pltpu.SemaphoreType.DMA((RING - 1,))],
        cost_estimate=pl.CostEstimate(
            flops=0, bytes_accessed=4 * blocks[0].size, transcendentals=0
        ),
        compiler_params=params(24),
    )(*blocks)


def merge_kernel(z_first, hints, *refs):
    refs = refs[hints:]
    rows, table, sums, stage, table_sem, sems = refs[-6:]
    ins, outs = (refs[: RING + 2], refs[RING + 2 : -6]) if z_first else (refs[:1], refs[1:-6])
    sources = [(ref, j) for ref in ins for j in range(ref.shape[0])]
    pairs = ins[0].shape[1] - 1
    here = lax.axis_index("z")
    for i, (ref, j) in enumerate(sources):
        t = ref[j, pairs, 0, :, :128].astype(F32)[:8].astype(jnp.int32)
        if z_first:
            t = (((t >> 5) - here) & 7) * 32 + (t & 31)
        else:
            t = ((t >> 3) & 3) * 64 + (t >> 5) * 8 + (t & 7)
        rows[8 * i : 8 * i + 8, :] = t
    copy = pltpu.make_async_copy(rows, table, table_sem)
    copy.start()
    sums[...] = jnp.zeros_like(sums)
    copy.wait()
    for i, (ref, j) in enumerate(sources):

        def add_line(w, carry, i=i, ref=ref, j=j):
            for s in range(8):
                sums[table[8 * i + w, s]] += ref[j, w * 8 + s].astype(F32)
            return carry

        lax.fori_loop(0, pairs // 8, add_line, 0)
    some = sums.shape[0] // STEPS
    copies = []
    for n in range(STEPS):
        part = pl.ds(n * some, some)
        stage[part] = sums[part].astype(BF16)
        if not z_first:
            pieces = [(part, outs[0].at[part])]
        elif n == 4:
            pieces = [(pl.ds((8 + m) * some // 2, some // 2), outs[1 + m]) for m in range(2)]
        else:
            pieces = [(part, outs[0].at[n])]
        for source, out in pieces:
            copies.append(pltpu.make_async_copy(stage.at[source], out, sems.at[len(copies)]))
            copies[-1].start()
    for copy in copies:
        copy.wait()


def merge(hints, blocks, sectors, z_first):
    block = blocks[0].shape[2:]
    shapes = [(8, 32), (16,), (16,)] if z_first else [(sectors,)]
    full = pl.BlockSpec(blocks[-1].shape, lambda i: (0, 0, 0, 0, 0))
    own = pl.BlockSpec((1, *blocks[-1].shape[1:]), lambda i: (0, 0, 0, 0, 0))
    return pl.pallas_call(
        functools.partial(merge_kernel, z_first, len(hints)),
        grid=(1,),
        in_specs=[ANY] * len(hints) + [own] * (len(blocks) - 1) + [full],
        out_specs=[HBM] * len(shapes),
        out_shape=[jax.ShapeDtypeStruct((*shape, *block), BF16) for shape in shapes],
        scratch_shapes=[
            pltpu.VMEM((GROUPS * 8, 128), jnp.int32),
            pltpu.SMEM((GROUPS * 8, 128), jnp.int32),
            pltpu.VMEM((sectors, *block), F32),
            pltpu.VMEM((sectors, *block), BF16),
            pltpu.SemaphoreType.DMA,
            pltpu.SemaphoreType.DMA((STEPS + 1,)),
        ],
        cost_estimate=pl.CostEstimate(flops=2**22, bytes_accessed=2**23, transcendentals=0),
        compiler_params=params(56),
    )(*hints, *blocks)


def join_kernel(first, up_base, down_base, up, down, up_out, down_out):
    half = up.shape[0]
    if first:
        up_out[:half] = (up_base[0, :half].astype(F32) + up[...].astype(F32)).astype(BF16)
        up_out[half:] = up_base[0, half:]
        down_out[:half] = down_base[0, :half]
        down_out[half:] = (down_base[0, half:].astype(F32) + down[...].astype(F32)).astype(BF16)
    else:
        up_out[...] = (up_base[0].astype(F32) + up[...].astype(F32)).astype(BF16)
        down_out[...] = (down_base[0].astype(F32) + down[...].astype(F32)).astype(BF16)


def join(dense, near, up, down):
    shape = dense.shape[1:]
    first = up.shape[0] != shape[0]

    def pick(n):
        return pl.BlockSpec((1, *shape), lambda i: (n, 0, 0, 0, 0))

    return pl.pallas_call(
        functools.partial(join_kernel, first),
        grid=(1,),
        in_specs=[pick(near), pick(8 - near), VMEM, VMEM],
        out_specs=[VMEM] * 2,
        out_shape=[jax.ShapeDtypeStruct(shape, BF16)] * 2,
        cost_estimate=pl.CostEstimate(flops=2**20, bytes_accessed=2**21, transcendentals=0),
        compiler_params=params(16),
    )(dense, dense, up, down)


def settle_kernel(own, up, down, *parts):
    here = parts[0].shape[0]
    y = lax.axis_index("y")
    for k in range(RING):
        rows = pl.ds(pl.multiple_of((y + k) % RING * here, here), here)
        total = own[0, rows].astype(F32) + up[rows].astype(F32) + down[rows].astype(F32)
        parts[k][...] = total.astype(BF16)


def settle(dense, up, down):
    count, *rest = dense.shape[1:]
    return pl.pallas_call(
        settle_kernel,
        grid=(1,),
        in_specs=[pl.BlockSpec((1, count, *rest), lambda i: (0, 0, 0, 0, 0)), VMEM, VMEM],
        out_specs=[VMEM] * RING,
        out_shape=[jax.ShapeDtypeStruct((count // RING, *rest), BF16)] * RING,
        cost_estimate=pl.CostEstimate(flops=2**20, bytes_accessed=2**21, transcendentals=0),
        compiler_params=params(16),
    )(dense, up, down)


def reduce_kernel(blocks, out, stage, sems):
    step = pl.program_id(0)
    some = blocks.shape[1]

    def copy(i):
        part = pl.ds(i * some, some)
        return pltpu.make_async_copy(stage.at[part], out.at[part], sems.at[i])

    total = sum(blocks[x].astype(F32) for x in range(RING))
    stage[pl.ds(step * some, some)] = total.astype(BF16)
    copy(step).start()

    @pl.when(step == pl.num_programs(0) - 1)
    def _():
        for i in range(4):
            copy(i).wait()


def reduce(blocks):
    _, count, *rest = blocks.shape
    steps = 4
    return pl.pallas_call(
        reduce_kernel,
        grid=(steps,),
        in_specs=[pl.BlockSpec((RING, count // steps, *rest), lambda i: (0, i, 0, 0, 0))],
        out_specs=HBM,
        out_shape=jax.ShapeDtypeStruct((count, *rest), BF16),
        scratch_shapes=[
            pltpu.VMEM((count, *rest), BF16),
            pltpu.SemaphoreType.DMA((steps,)),
        ],
        cost_estimate=pl.CostEstimate(flops=2**22, bytes_accessed=2**22, transcendentals=0),
        compiler_params=params(16),
    )(blocks)


def gate(x, *waits):
    return pl.pallas_call(
        lambda *refs: None,
        in_specs=[HBM] + [ANY] * len(waits),
        out_specs=HBM,
        out_shape=jax.ShapeDtypeStruct(x.shape, x.dtype),
        input_output_aliases={0: 0},
        compiler_params=params(62),
    )(x, *waits)


def finish_kernel(scale, first, second, local, trial_rows, out, gram):
    size = out.shape[-1]
    found = [[jnp.zeros((SUB, size), F32) for _ in range(2)] for _ in range(2)]
    for half in range(2):
        rows = slice(half * SUB, (half + 1) * SUB)
        for b in range(2):
            if half == 0:
                total = first[:, b].astype(F32)
            else:
                total = sum(second[z, :, b].astype(F32) for z in range(second.shape[0]))
            total = total + local[b, :, rows]
            out[b, :, rows] = total.astype(BF16)
            for a in range(2):
                found[a][b] += jnp.sum(trial_rows[a, :, rows].astype(F32) * total, axis=0)
    for a in range(2):
        for b in range(2):
            gram[a, b] = jnp.sum(found[a][b]) * scale


def finish(scale, *args):
    local = args[2]
    return pl.pallas_call(
        functools.partial(finish_kernel, scale),
        in_specs=[VMEM] * 4,
        out_specs=[VMEM, SMEM],
        out_shape=[
            jax.ShapeDtypeStruct(local.shape, BF16),
            jax.ShapeDtypeStruct((2, 2), F32),
        ],
        cost_estimate=pl.CostEstimate(flops=2**21, bytes_accessed=2**21, transcendentals=0),
        compiler_params=params(24),
    )(*args)


def to_all(x, axes):
    return lax.all_to_all(x, axes, 0, 0, tiled=True)


def spread(x, axes):
    return to_all(jnp.broadcast_to(x[None], (lax.axis_size(axes), *x.shape)), axes)


def shift(x, axis, k):
    n = lax.axis_size(axis)
    return lax.ppermute(x, axis, [(i, (i + k) % n) for i in range(n)])


def swap(x):
    return lax.ppermute(x, "core", [(0, 1), (1, 0)])


def turn(x, k):
    pairs = [
        (a * RING + b, (b + k) % RING * RING + a) for a in range(RING) for b in range(RING)
    ]
    return lax.ppermute(x, ("x", "y"), pairs)


def add(*arrays):
    return sum(x.astype(F32) for x in arrays).astype(BF16)


def body(trial, left_env, right_env, left_block_ham, right_block_ham, target):
    op = ("y", "core")
    nz, nx = lax.axis_size("z"), lax.axis_size("x")
    terms, here, size, _ = left_env.shape
    sectors = nz * nx * here
    rows = size // lax.axis_size(op)
    first_row = lax.axis_index(op) * rows
    trial_rows = lax.dynamic_slice_in_dim(trial, first_row, rows, 2)
    local = jnp.einsum("sij,vsjk->vsik", left_block_ham, trial, preferred_element_type=F32)
    local = local + jnp.einsum(
        "vsij,sjk->vsik", trial_rows, right_block_ham, preferred_element_type=F32
    )

    pieces, mine, other, *strips = contract(target, trial, left_env, right_env)
    pieces = to_all(pieces, op)
    strips = [shift(strip, "x", k) for k, strip in enumerate(strips, 1)]
    others, hint = pack(strips)
    got = swap(other)

    (blocks,) = merge([hint, got], [pieces], sectors, False)
    dense, up, down = merge([blocks], [mine, got, *strips, swap(others)], sectors, True)
    blocks = to_all(blocks.reshape(nx, nz * here, 2, SUB, size), "x")
    for near in (3, 2, 1):
        up, down = join(dense, near, shift(up, "z", 1), shift(down, "z", -1))
    up, down = shift(up, "z", 1), shift(down, "z", -1)
    halves = gate(reduce(blocks), up, down)
    second = to_all(halves.reshape(nz, here, 2, SUB, size), "z")
    parts = settle(dense, up, down)

    first = add(*(turn(parts[k], k) for k in range(RING)))

    scale = 1.0 / (sectors * size * size)
    hpsi, gram = finish(scale, first, second, local, trial_rows)
    gram = jnp.sum(spread(gram, ("z", "x")), axis=0)
    gram = jnp.sum(spread(gram, op), axis=0)
    return hpsi, gram


def solution(mesh):
    sizes = {"z": 8, "x": 4, "y": 4, "core": 2}
    fine = Mesh(mesh.devices.reshape(tuple(sizes.values())), tuple(sizes))
    sec, op = ("z", "x"), ("y", "core")
    return jax.shard_map(
        body,
        mesh=fine,
        in_specs=(
            P(None, sec, None, None),
            P(op, sec, None, None),
            P(op, sec, None, None),
            P(sec, op, None),
            P(sec, None, None),
            P(op, sec),
        ),
        out_specs=(P(None, sec, op, None), P()),
        check_vma=False,
    )
```

```python
import functools

import jax
import jax.numpy as jnp
from jax import lax
from jax.experimental import pallas as pl
from jax.experimental.pallas import tpu as pltpu
from jax.sharding import Mesh
from jax.sharding import PartitionSpec as P

BF16 = jnp.bfloat16
F32 = jnp.float32
RING = 4
GROUPS = 8
SUB = 16
STEPS = 8
VMEM = pl.BlockSpec(memory_space=pltpu.VMEM)
SMEM = pl.BlockSpec(memory_space=pltpu.SMEM)
HBM = pl.BlockSpec(memory_space=pltpu.HBM)
ANY = pl.BlockSpec(memory_space=pl.ANY)
HINT = jax.ShapeDtypeStruct((8, 128), F32)


def params(mib):
    return pltpu.CompilerParams(vmem_limit_bytes=mib * 2**20)


def contract_kernel(target_ref, left_ref, right_ref, trial_ref, *refs):
    outs, (stage, slab, wide, sems, slab_sems) = refs[: 2 + RING], refs[2 + RING :]
    step = pl.program_id(0)
    last = pl.num_programs(0) - 1
    here, size = left_ref.shape[1], left_ref.shape[3]
    x, core = lax.axis_index("x"), lax.axis_index("core")
    order = [SUB * (2 * r + 1) for r in range(GROUPS)]
    order += [
        pl.multiple_of(((x + k) % RING * 2 + c) * 2 * SUB, SUB)
        for k in range(RING)
        for c in (core, 1 - core)
    ]
    places = [(0, GROUPS), (GROUPS, 1), (GROUPS + 1, 1)]
    places += [(GROUPS + 2 * k, 2) for k in range(1, RING)]

    def copies(i):
        rows = pl.ds(i * here, here)
        return [
            pltpu.make_async_copy(
                stage.at[i % 2, pl.ds(a, n)], out.at[:, rows], sems.at[i % 2, j]
            )
            for j, (out, (a, n)) in enumerate(zip(outs, places, strict=True))
        ]

    def slab_copies():
        return [
            pltpu.make_async_copy(
                slab.at[pl.ds(0, n)], out.at[:, pl.ds(here * (last + 1), 1)], slab_sems.at[j]
            )
            for j, (out, (_, n)) in enumerate(zip(outs, places, strict=True))
        ]

    @pl.when(step == 0)
    def _():
        wide[...] = jnp.zeros_like(wide)
        wide[:4, :8] = target_ref[...].astype(F32)
        for g in range(GROUPS):
            for v in range(2):
                slab[g, 0, v] = wide[...].astype(BF16)
        for copy in slab_copies():
            copy.start()

    @pl.when(step >= 2)
    def _():
        for copy in copies(step - 2):
            copy.wait()

    for s in range(here):
        rows = jnp.concatenate([left_ref[0, s, pl.ds(a, SUB), :] for a in order], axis=0)
        both = jnp.concatenate([trial_ref[0, s], trial_ref[1, s]], axis=1)
        half = jnp.dot(rows, both, preferred_element_type=F32).astype(BF16)
        half = jnp.concatenate([half[:, :size], half[:, size:]], axis=0)
        piece = jnp.dot(half, right_ref[0, s], preferred_element_type=F32).astype(BF16)
        piece = piece.reshape(2, 2 * GROUPS, SUB, size)
        for v in range(2):
            stage[step % 2, :, s, v] = piece[v]
    for copy in copies(step):
        copy.start()

    @pl.when(step == last)
    def _():
        for copy in copies(step - 1) + copies(step) + slab_copies():
            copy.wait()


def contract(target, trial, left_env, right_env):
    terms, here, size, _ = left_env.shape
    shapes = [(n, terms * here + 1, 2, SUB, size) for n in (GROUPS, 1, 1, 2, 2, 2)]
    return pl.pallas_call(
        contract_kernel,
        grid=(terms,),
        in_specs=[
            VMEM,
            pl.BlockSpec((1, here, size, size), lambda w: (w, 0, 0, 0)),
            pl.BlockSpec((1, here, size, size), lambda w: (w, 0, 0, 0)),
            pl.BlockSpec((2, here, size, size), lambda w: (0, 0, 0, 0)),
        ],
        out_specs=[HBM] * len(shapes),
        out_shape=[jax.ShapeDtypeStruct(shape, BF16) for shape in shapes],
        scratch_shapes=[
            pltpu.VMEM((2, 2 * GROUPS, here, 2, SUB, size), BF16),
            pltpu.VMEM((GROUPS, 1, 2, SUB, size), BF16),
            pltpu.VMEM((SUB, size), F32),
            pltpu.SemaphoreType.DMA((2, len(shapes))),
            pltpu.SemaphoreType.DMA((len(shapes),)),
        ],
        cost_estimate=pl.CostEstimate(
            flops=8 * terms * here * size**3,
            bytes_accessed=8 * terms * here * size * size,
            transcendentals=0,
        ),
        compiler_params=params(56),
    )(target, left_env, right_env, trial)


def pack_kernel(*refs):
    ins, (out, hint, sems) = refs[: RING - 1], refs[RING - 1 :]
    hint[...] = jnp.zeros_like(hint)
    copies = [
        pltpu.make_async_copy(ref.at[1], out.at[k], sems.at[k]) for k, ref in enumerate(ins)
    ]
    for copy in copies:
        copy.start()
    for copy in copies:
        copy.wait()


def pack(blocks):
    shape = blocks[0].shape[1:]
    return pl.pallas_call(
        pack_kernel,
        in_specs=[HBM] * (RING - 1),
        out_specs=[HBM, VMEM],
        out_shape=[jax.ShapeDtypeStruct((RING - 1, *shape), BF16), HINT],
        scratch_shapes=[pltpu.SemaphoreType.DMA((RING - 1,))],
        cost_estimate=pl.CostEstimate(
            flops=0, bytes_accessed=4 * blocks[0].size, transcendentals=0
        ),
        compiler_params=params(24),
    )(*blocks)


def merge_kernel(z_first, hints, *refs):
    refs = refs[hints:]
    rows, table, sums, stage, table_sem, sems = refs[-6:]
    ins, outs = (refs[: RING + 2], refs[RING + 2 : -6]) if z_first else (refs[:1], refs[1:-6])
    sources = [(ref, j) for ref in ins for j in range(ref.shape[0])]
    pairs = ins[0].shape[1] - 1
    here = lax.axis_index("z")
    for i, (ref, j) in enumerate(sources):
        t = ref[j, pairs, 0, :, :128].astype(F32)[:8].astype(jnp.int32)
        if z_first:
            t = (((t >> 5) - here) & 7) * 32 + (t & 31)
        else:
            t = ((t >> 3) & 3) * 64 + (t >> 5) * 8 + (t & 7)
        rows[8 * i : 8 * i + 8, :] = t
    copy = pltpu.make_async_copy(rows, table, table_sem)
    copy.start()
    sums[...] = jnp.zeros_like(sums)
    copy.wait()
    for i, (ref, j) in enumerate(sources):

        def add_line(w, carry, i=i, ref=ref, j=j):
            for s in range(8):
                sums[table[8 * i + w, s]] += ref[j, w * 8 + s].astype(F32)
            return carry

        lax.fori_loop(0, pairs // 8, add_line, 0)
    some = sums.shape[0] // STEPS
    copies = []
    for n in range(STEPS):
        part = pl.ds(n * some, some)
        stage[part] = sums[part].astype(BF16)
        if not z_first:
            pieces = [(part, outs[0].at[part])]
        elif n == 4:
            pieces = [(pl.ds((8 + m) * some // 2, some // 2), outs[1 + m]) for m in range(2)]
        else:
            pieces = [(part, outs[0].at[n])]
        for source, out in pieces:
            copies.append(pltpu.make_async_copy(stage.at[source], out, sems.at[len(copies)]))
            copies[-1].start()
    for copy in copies:
        copy.wait()


def merge(hints, blocks, sectors, z_first):
    block = blocks[0].shape[2:]
    shapes = [(8, 32), (16,), (16,)] if z_first else [(sectors,)]
    full = pl.BlockSpec(blocks[-1].shape, lambda i: (0, 0, 0, 0, 0))
    own = pl.BlockSpec((1, *blocks[-1].shape[1:]), lambda i: (0, 0, 0, 0, 0))
    return pl.pallas_call(
        functools.partial(merge_kernel, z_first, len(hints)),
        grid=(1,),
        in_specs=[ANY] * len(hints) + [own] * (len(blocks) - 1) + [full],
        out_specs=[HBM] * len(shapes),
        out_shape=[jax.ShapeDtypeStruct((*shape, *block), BF16) for shape in shapes],
        scratch_shapes=[
            pltpu.VMEM((GROUPS * 8, 128), jnp.int32),
            pltpu.SMEM((GROUPS * 8, 128), jnp.int32),
            pltpu.VMEM((sectors, *block), F32),
            pltpu.VMEM((sectors, *block), BF16),
            pltpu.SemaphoreType.DMA,
            pltpu.SemaphoreType.DMA((STEPS + 1,)),
        ],
        cost_estimate=pl.CostEstimate(flops=2**22, bytes_accessed=2**23, transcendentals=0),
        compiler_params=params(56),
    )(*hints, *blocks)


def join_kernel(side, base, extra, out):
    half = extra.shape[0]
    if side == 0:
        out[...] = (base[0].astype(F32) + extra[...].astype(F32)).astype(BF16)
        return
    mixed = slice(0, half) if side == 1 else slice(half, None)
    kept = slice(half, None) if side == 1 else slice(0, half)
    out[mixed] = (base[0, mixed].astype(F32) + extra[...].astype(F32)).astype(BF16)
    out[kept] = base[0, kept]


def join(dense, n, extra):
    shape = dense.shape[1:]
    side = 0 if extra.shape[0] == shape[0] else 1 if n < 4 else 2
    return pl.pallas_call(
        functools.partial(join_kernel, side),
        grid=(1,),
        in_specs=[pl.BlockSpec((1, *shape), lambda i: (n, 0, 0, 0, 0)), VMEM],
        out_specs=VMEM,
        out_shape=jax.ShapeDtypeStruct(shape, BF16),
        cost_estimate=pl.CostEstimate(flops=2**20, bytes_accessed=2**21, transcendentals=0),
        compiler_params=params(16),
    )(dense, extra)


def settle_kernel(own, up, down, *parts):
    here = parts[0].shape[0]
    y = lax.axis_index("y")
    for k in range(RING):
        rows = pl.ds(pl.multiple_of((y + k) % RING * here, here), here)
        total = own[0, rows].astype(F32) + up[rows].astype(F32) + down[rows].astype(F32)
        parts[k][...] = total.astype(BF16)


def settle(dense, up, down):
    count, *rest = dense.shape[1:]
    return pl.pallas_call(
        settle_kernel,
        grid=(1,),
        in_specs=[pl.BlockSpec((1, count, *rest), lambda i: (0, 0, 0, 0, 0)), VMEM, VMEM],
        out_specs=[VMEM] * RING,
        out_shape=[jax.ShapeDtypeStruct((count // RING, *rest), BF16)] * RING,
        cost_estimate=pl.CostEstimate(flops=2**20, bytes_accessed=2**21, transcendentals=0),
        compiler_params=params(16),
    )(dense, up, down)


def reduce_kernel(blocks, out, stage, sems):
    step = pl.program_id(0)
    some = blocks.shape[1]

    def copy(i):
        part = pl.ds(i * some, some)
        return pltpu.make_async_copy(stage.at[part], out.at[part], sems.at[i])

    total = sum(blocks[x].astype(F32) for x in range(RING))
    stage[pl.ds(step * some, some)] = total.astype(BF16)
    copy(step).start()

    @pl.when(step == pl.num_programs(0) - 1)
    def _():
        for i in range(4):
            copy(i).wait()


def reduce(blocks):
    _, count, *rest = blocks.shape
    steps = 4
    return pl.pallas_call(
        reduce_kernel,
        grid=(steps,),
        in_specs=[pl.BlockSpec((RING, count // steps, *rest), lambda i: (0, i, 0, 0, 0))],
        out_specs=HBM,
        out_shape=jax.ShapeDtypeStruct((count, *rest), BF16),
        scratch_shapes=[
            pltpu.VMEM((count, *rest), BF16),
            pltpu.SemaphoreType.DMA((steps,)),
        ],
        cost_estimate=pl.CostEstimate(flops=2**22, bytes_accessed=2**22, transcendentals=0),
        compiler_params=params(16),
    )(blocks)


def gate(x, *waits):
    return pl.pallas_call(
        lambda *refs: None,
        in_specs=[HBM] + [ANY] * len(waits),
        out_specs=HBM,
        out_shape=jax.ShapeDtypeStruct(x.shape, x.dtype),
        input_output_aliases={0: 0},
        compiler_params=params(62),
    )(x, *waits)


def finish_kernel(scale, first, second, local, trial_rows, out, gram):
    size = out.shape[-1]
    found = [[jnp.zeros((SUB, size), F32) for _ in range(2)] for _ in range(2)]
    for half in range(2):
        rows = slice(half * SUB, (half + 1) * SUB)
        for b in range(2):
            if half == 0:
                total = first[:, b].astype(F32)
            else:
                total = sum(second[z, :, b].astype(F32) for z in range(second.shape[0]))
            total = total + local[b, :, rows]
            out[b, :, rows] = total.astype(BF16)
            for a in range(2):
                found[a][b] += jnp.sum(trial_rows[a, :, rows].astype(F32) * total, axis=0)
    for a in range(2):
        for b in range(2):
            gram[a, b] = jnp.sum(found[a][b]) * scale


def finish(scale, *args):
    local = args[2]
    return pl.pallas_call(
        functools.partial(finish_kernel, scale),
        in_specs=[VMEM] * 4,
        out_specs=[VMEM, SMEM],
        out_shape=[
            jax.ShapeDtypeStruct(local.shape, BF16),
            jax.ShapeDtypeStruct((2, 2), F32),
        ],
        cost_estimate=pl.CostEstimate(flops=2**21, bytes_accessed=2**21, transcendentals=0),
        compiler_params=params(24),
    )(*args)


def to_all(x, axes):
    return lax.all_to_all(x, axes, 0, 0, tiled=True)


def spread(x, axes):
    return to_all(jnp.broadcast_to(x[None], (lax.axis_size(axes), *x.shape)), axes)


def shift(x, axis, k):
    n = lax.axis_size(axis)
    return lax.ppermute(x, axis, [(i, (i + k) % n) for i in range(n)])


def swap(x):
    return lax.ppermute(x, "core", [(0, 1), (1, 0)])


def turn(x, k):
    pairs = [
        (a * RING + b, (b + k) % RING * RING + a) for a in range(RING) for b in range(RING)
    ]
    return lax.ppermute(x, ("x", "y"), pairs)


def add(*arrays):
    return sum(x.astype(F32) for x in arrays).astype(BF16)


def body(trial, left_env, right_env, left_block_ham, right_block_ham, target):
    op = ("y", "core")
    nz, nx = lax.axis_size("z"), lax.axis_size("x")
    terms, here, size, _ = left_env.shape
    sectors = nz * nx * here
    rows = size // lax.axis_size(op)
    first_row = lax.axis_index(op) * rows
    trial_rows = lax.dynamic_slice_in_dim(trial, first_row, rows, 2)
    local = jnp.einsum("sij,vsjk->vsik", left_block_ham, trial, preferred_element_type=F32)
    local = local + jnp.einsum(
        "vsij,sjk->vsik", trial_rows, right_block_ham, preferred_element_type=F32
    )

    pieces, mine, other, *strips = contract(target, trial, left_env, right_env)
    pieces = to_all(pieces, op)
    strips = [shift(strip, "x", k) for k, strip in enumerate(strips, 1)]
    others, hint = pack(strips)
    got = swap(other)

    (blocks,) = merge([hint, got], [pieces], sectors, False)
    dense, up, down = merge([blocks], [mine, got, *strips, swap(others)], sectors, True)
    blocks = to_all(blocks.reshape(nx, nz * here, 2, SUB, size), "x")
    for near in (3, 2, 1):
        up, down = shift(up, "z", 1), shift(down, "z", -1)
        up, down = join(dense, near, up), join(dense, 8 - near, down)
    up, down = shift(up, "z", 1), shift(down, "z", -1)
    halves = gate(reduce(blocks), up, down)
    second = to_all(halves.reshape(nz, here, 2, SUB, size), "z")
    parts = settle(dense, up, down)

    first = add(*(turn(parts[k], k) for k in range(RING)))

    scale = 1.0 / (sectors * size * size)
    hpsi, gram = finish(scale, first, second, local, trial_rows)
    gram = jnp.sum(spread(gram, ("y", "core")), axis=0)
    gram = jnp.sum(spread(gram, ("z", "x")), axis=0)
    return hpsi, gram


def solution(mesh):
    sizes = {"z": 8, "x": 4, "y": 4, "core": 2}
    fine = Mesh(mesh.devices.reshape(tuple(sizes.values())), tuple(sizes))
    sec, op = ("z", "x"), ("y", "core")
    return jax.shard_map(
        body,
        mesh=fine,
        in_specs=(
            P(None, sec, None, None),
            P(op, sec, None, None),
            P(op, sec, None, None),
            P(sec, op, None),
            P(sec, None, None),
            P(op, sec),
        ),
        out_specs=(P(None, sec, op, None), P()),
        check_vma=False,
    )
```

```python
import functools

import jax
import jax.numpy as jnp
from jax import lax
from jax.experimental import pallas as pl
from jax.experimental.pallas import tpu as pltpu
from jax.sharding import Mesh
from jax.sharding import PartitionSpec as P

BF16 = jnp.bfloat16
F32 = jnp.float32
RING = 4
GROUPS = 8
SUB = 16
STEPS = 8
VMEM = pl.BlockSpec(memory_space=pltpu.VMEM)
SMEM = pl.BlockSpec(memory_space=pltpu.SMEM)
HBM = pl.BlockSpec(memory_space=pltpu.HBM)
ANY = pl.BlockSpec(memory_space=pl.ANY)
HINT = jax.ShapeDtypeStruct((8, 128), F32)


def params(mib):
    return pltpu.CompilerParams(vmem_limit_bytes=mib * 2**20)


def contract_kernel(target_ref, left_ref, right_ref, trial_ref, *refs):
    outs, (stage, slab, wide, sems, slab_sems) = refs[: 2 + RING], refs[2 + RING :]
    step = pl.program_id(0)
    last = pl.num_programs(0) - 1
    here, size = left_ref.shape[1], left_ref.shape[3]
    x, core = lax.axis_index("x"), lax.axis_index("core")
    order = [SUB * (2 * r + 1) for r in range(GROUPS)]
    order += [
        pl.multiple_of(((x + k) % RING * 2 + c) * 2 * SUB, SUB)
        for k in range(RING)
        for c in (core, 1 - core)
    ]
    places = [(0, GROUPS), (GROUPS, 1), (GROUPS + 1, 1)]
    places += [(GROUPS + 2 * k, 2) for k in range(1, RING)]

    def copies(i):
        rows = pl.ds(i * here, here)
        return [
            pltpu.make_async_copy(
                stage.at[i % 2, pl.ds(a, n)], out.at[:, rows], sems.at[i % 2, j]
            )
            for j, (out, (a, n)) in enumerate(zip(outs, places, strict=True))
        ]

    def slab_copies():
        return [
            pltpu.make_async_copy(
                slab.at[pl.ds(0, n)], out.at[:, pl.ds(here * (last + 1), 1)], slab_sems.at[j]
            )
            for j, (out, (_, n)) in enumerate(zip(outs, places, strict=True))
        ]

    @pl.when(step == 0)
    def _():
        wide[...] = jnp.zeros_like(wide)
        wide[:4, :8] = target_ref[...].astype(F32)
        for g in range(GROUPS):
            for v in range(2):
                slab[g, 0, v] = wide[...].astype(BF16)
        for copy in slab_copies():
            copy.start()

    @pl.when(step >= 2)
    def _():
        for copy in copies(step - 2):
            copy.wait()

    for s in range(here):
        rows = jnp.concatenate([left_ref[0, s, pl.ds(a, SUB), :] for a in order], axis=0)
        both = jnp.concatenate([trial_ref[0, s], trial_ref[1, s]], axis=1)
        half = jnp.dot(rows, both, preferred_element_type=F32).astype(BF16)
        half = jnp.concatenate([half[:, :size], half[:, size:]], axis=0)
        piece = jnp.dot(half, right_ref[0, s], preferred_element_type=F32).astype(BF16)
        piece = piece.reshape(2, 2 * GROUPS, SUB, size)
        for v in range(2):
            stage[step % 2, :, s, v] = piece[v]
    for copy in copies(step):
        copy.start()

    @pl.when(step == last)
    def _():
        for copy in copies(step - 1) + copies(step) + slab_copies():
            copy.wait()


def contract(target, trial, left_env, right_env):
    terms, here, size, _ = left_env.shape
    shapes = [(n, terms * here + 1, 2, SUB, size) for n in (GROUPS, 1, 1, 2, 2, 2)]
    return pl.pallas_call(
        contract_kernel,
        grid=(terms,),
        in_specs=[
            VMEM,
            pl.BlockSpec((1, here, size, size), lambda w: (w, 0, 0, 0)),
            pl.BlockSpec((1, here, size, size), lambda w: (w, 0, 0, 0)),
            pl.BlockSpec((2, here, size, size), lambda w: (0, 0, 0, 0)),
        ],
        out_specs=[HBM] * len(shapes),
        out_shape=[jax.ShapeDtypeStruct(shape, BF16) for shape in shapes],
        scratch_shapes=[
            pltpu.VMEM((2, 2 * GROUPS, here, 2, SUB, size), BF16),
            pltpu.VMEM((GROUPS, 1, 2, SUB, size), BF16),
            pltpu.VMEM((SUB, size), F32),
            pltpu.SemaphoreType.DMA((2, len(shapes))),
            pltpu.SemaphoreType.DMA((len(shapes),)),
        ],
        cost_estimate=pl.CostEstimate(
            flops=8 * terms * here * size**3,
            bytes_accessed=8 * terms * here * size * size,
            transcendentals=0,
        ),
        compiler_params=params(56),
    )(target, left_env, right_env, trial)


def pack_kernel(*refs):
    ins, (out, hint, sems) = refs[: RING - 1], refs[RING - 1 :]
    hint[...] = jnp.zeros_like(hint)
    copies = [
        pltpu.make_async_copy(ref.at[1], out.at[k], sems.at[k]) for k, ref in enumerate(ins)
    ]
    for copy in copies:
        copy.start()
    for copy in copies:
        copy.wait()


def pack(blocks):
    shape = blocks[0].shape[1:]
    return pl.pallas_call(
        pack_kernel,
        in_specs=[HBM] * (RING - 1),
        out_specs=[HBM, VMEM],
        out_shape=[jax.ShapeDtypeStruct((RING - 1, *shape), BF16), HINT],
        scratch_shapes=[pltpu.SemaphoreType.DMA((RING - 1,))],
        cost_estimate=pl.CostEstimate(
            flops=0, bytes_accessed=4 * blocks[0].size, transcendentals=0
        ),
        compiler_params=params(24),
    )(*blocks)


def merge_kernel(z_first, hints, *refs):
    refs = refs[hints:]
    buf, in_sems, rows, table, sums, stage, table_sem, sems = refs[-8:]
    ins, outs = (refs[: RING + 2], refs[RING + 2 : -8]) if z_first else (refs[:1], refs[1:-8])
    counts = [1] * (RING + 1) + [RING - 1] if z_first else [GROUPS]
    given = [(ref, j) for ref, n in zip(ins, counts, strict=True) for j in range(n)]
    loads = [
        pltpu.make_async_copy(ref.at[j], buf.at[i], in_sems.at[i])
        for i, (ref, j) in enumerate(given)
    ]
    for load in loads:
        load.start()
    sums[...] = jnp.zeros_like(sums)
    for load in loads:
        load.wait()
    sources = [(buf, i) for i in range(GROUPS)]
    pairs = buf.shape[1] - 1
    here = lax.axis_index("z")
    for i, (ref, j) in enumerate(sources):
        t = ref[j, pairs, 0, :, :128].astype(F32)[:8].astype(jnp.int32)
        if z_first:
            t = (((t >> 5) - here) & 7) * 32 + (t & 31)
        else:
            t = ((t >> 3) & 3) * 64 + (t >> 5) * 8 + (t & 7)
        rows[8 * i : 8 * i + 8, :] = t
    copy = pltpu.make_async_copy(rows, table, table_sem)
    copy.start()
    copy.wait()
    for i, (ref, j) in enumerate(sources):

        def add_line(w, carry, i=i, ref=ref, j=j):
            for s in range(8):
                sums[table[8 * i + w, s]] += ref[j, w * 8 + s].astype(F32)
            return carry

        lax.fori_loop(0, pairs // 8, add_line, 0)
    some = sums.shape[0] // STEPS
    copies = []
    for n in range(STEPS):
        part = pl.ds(n * some, some)
        stage[part] = sums[part].astype(BF16)
        if not z_first:
            pieces = [(part, outs[0].at[part])]
        elif n == 4:
            pieces = [(pl.ds((8 + m) * some // 2, some // 2), outs[1 + m]) for m in range(2)]
        else:
            pieces = [(part, outs[0].at[n])]
        for source, out in pieces:
            copies.append(pltpu.make_async_copy(stage.at[source], out, sems.at[len(copies)]))
            copies[-1].start()
    for copy in copies:
        copy.wait()


def merge(hints, blocks, sectors, z_first):
    block = blocks[0].shape[2:]
    shapes = [(8, 32), (16,), (16,)] if z_first else [(sectors,)]
    full = pl.BlockSpec(blocks[-1].shape, lambda i: (0, 0, 0, 0, 0))
    own = pl.BlockSpec((1, *blocks[-1].shape[1:]), lambda i: (0, 0, 0, 0, 0))
    return pl.pallas_call(
        functools.partial(merge_kernel, z_first, len(hints)),
        grid=(1,),
        in_specs=[ANY] * len(hints) + [HBM] * len(blocks),
        out_specs=[HBM] * len(shapes),
        out_shape=[jax.ShapeDtypeStruct((*shape, *block), BF16) for shape in shapes],
        scratch_shapes=[
            pltpu.VMEM((GROUPS, *blocks[-1].shape[1:]), BF16),
            pltpu.SemaphoreType.DMA((GROUPS,)),
            pltpu.VMEM((GROUPS * 8, 128), jnp.int32),
            pltpu.SMEM((GROUPS * 8, 128), jnp.int32),
            pltpu.VMEM((sectors, *block), F32),
            pltpu.VMEM((sectors, *block), BF16),
            pltpu.SemaphoreType.DMA,
            pltpu.SemaphoreType.DMA((STEPS + 1,)),
        ],
        cost_estimate=pl.CostEstimate(flops=2**22, bytes_accessed=2**23, transcendentals=0),
        compiler_params=params(56),
    )(*hints, *blocks)


def join_kernel(side, base, extra, out):
    half = extra.shape[0]
    if side == 0:
        out[...] = (base[0].astype(F32) + extra[...].astype(F32)).astype(BF16)
        return
    mixed = slice(0, half) if side == 1 else slice(half, None)
    kept = slice(half, None) if side == 1 else slice(0, half)
    out[mixed] = (base[0, mixed].astype(F32) + extra[...].astype(F32)).astype(BF16)
    out[kept] = base[0, kept]


def join(dense, n, extra):
    shape = dense.shape[1:]
    side = 0 if extra.shape[0] == shape[0] else 1 if n < 4 else 2
    return pl.pallas_call(
        functools.partial(join_kernel, side),
        grid=(1,),
        in_specs=[pl.BlockSpec((1, *shape), lambda i: (n, 0, 0, 0, 0)), VMEM],
        out_specs=VMEM,
        out_shape=jax.ShapeDtypeStruct(shape, BF16),
        cost_estimate=pl.CostEstimate(flops=2**20, bytes_accessed=2**21, transcendentals=0),
        compiler_params=params(16),
    )(dense, extra)


def settle_kernel(own, up, down, *parts):
    here = parts[0].shape[0]
    y = lax.axis_index("y")
    for k in range(RING):
        rows = pl.ds(pl.multiple_of((y + k) % RING * here, here), here)
        total = own[0, rows].astype(F32) + up[rows].astype(F32) + down[rows].astype(F32)
        parts[k][...] = total.astype(BF16)


def settle(dense, up, down):
    count, *rest = dense.shape[1:]
    return pl.pallas_call(
        settle_kernel,
        grid=(1,),
        in_specs=[pl.BlockSpec((1, count, *rest), lambda i: (0, 0, 0, 0, 0)), VMEM, VMEM],
        out_specs=[VMEM] * RING,
        out_shape=[jax.ShapeDtypeStruct((count // RING, *rest), BF16)] * RING,
        cost_estimate=pl.CostEstimate(flops=2**20, bytes_accessed=2**21, transcendentals=0),
        compiler_params=params(16),
    )(dense, up, down)


def reduce_kernel(blocks, out, stage, sems):
    step = pl.program_id(0)
    some = blocks.shape[1]

    def copy(i):
        part = pl.ds(i * some, some)
        return pltpu.make_async_copy(stage.at[part], out.at[part], sems.at[i])

    total = sum(blocks[x].astype(F32) for x in range(RING))
    stage[pl.ds(step * some, some)] = total.astype(BF16)
    copy(step).start()

    @pl.when(step == pl.num_programs(0) - 1)
    def _():
        for i in range(4):
            copy(i).wait()


def reduce(blocks):
    _, count, *rest = blocks.shape
    steps = 4
    return pl.pallas_call(
        reduce_kernel,
        grid=(steps,),
        in_specs=[pl.BlockSpec((RING, count // steps, *rest), lambda i: (0, i, 0, 0, 0))],
        out_specs=HBM,
        out_shape=jax.ShapeDtypeStruct((count, *rest), BF16),
        scratch_shapes=[
            pltpu.VMEM((count, *rest), BF16),
            pltpu.SemaphoreType.DMA((steps,)),
        ],
        cost_estimate=pl.CostEstimate(flops=2**22, bytes_accessed=2**22, transcendentals=0),
        compiler_params=params(16),
    )(blocks)


def gate(x, *waits):
    return pl.pallas_call(
        lambda *refs: None,
        in_specs=[HBM] + [ANY] * len(waits),
        out_specs=HBM,
        out_shape=jax.ShapeDtypeStruct(x.shape, x.dtype),
        input_output_aliases={0: 0},
        compiler_params=params(62),
    )(x, *waits)


def finish_kernel(scale, first, second, local, trial_rows, out, gram):
    size = out.shape[-1]
    found = [[jnp.zeros((SUB, size), F32) for _ in range(2)] for _ in range(2)]
    for half in range(2):
        rows = slice(half * SUB, (half + 1) * SUB)
        for b in range(2):
            if half == 0:
                total = first[:, b].astype(F32)
            else:
                total = sum(second[z, :, b].astype(F32) for z in range(second.shape[0]))
            total = total + local[b, :, rows]
            out[b, :, rows] = total.astype(BF16)
            for a in range(2):
                found[a][b] += jnp.sum(trial_rows[a, :, rows].astype(F32) * total, axis=0)
    for a in range(2):
        for b in range(2):
            gram[a, b] = jnp.sum(found[a][b]) * scale


def finish(scale, *args):
    local = args[2]
    return pl.pallas_call(
        functools.partial(finish_kernel, scale),
        in_specs=[VMEM] * 4,
        out_specs=[VMEM, SMEM],
        out_shape=[
            jax.ShapeDtypeStruct(local.shape, BF16),
            jax.ShapeDtypeStruct((2, 2), F32),
        ],
        cost_estimate=pl.CostEstimate(flops=2**21, bytes_accessed=2**21, transcendentals=0),
        compiler_params=params(24),
    )(*args)


def to_all(x, axes):
    return lax.all_to_all(x, axes, 0, 0, tiled=True)


def spread(x, axes):
    return to_all(jnp.broadcast_to(x[None], (lax.axis_size(axes), *x.shape)), axes)


def shift(x, axis, k):
    n = lax.axis_size(axis)
    return lax.ppermute(x, axis, [(i, (i + k) % n) for i in range(n)])


def swap(x):
    return lax.ppermute(x, "core", [(0, 1), (1, 0)])


def turn(x, k):
    pairs = [
        (a * RING + b, (b + k) % RING * RING + a) for a in range(RING) for b in range(RING)
    ]
    return lax.ppermute(x, ("x", "y"), pairs)


def add(*arrays):
    return sum(x.astype(F32) for x in arrays).astype(BF16)


def body(trial, left_env, right_env, left_block_ham, right_block_ham, target):
    op = ("y", "core")
    nz, nx = lax.axis_size("z"), lax.axis_size("x")
    terms, here, size, _ = left_env.shape
    sectors = nz * nx * here
    rows = size // lax.axis_size(op)
    first_row = lax.axis_index(op) * rows
    trial_rows = lax.dynamic_slice_in_dim(trial, first_row, rows, 2)
    local = jnp.einsum("sij,vsjk->vsik", left_block_ham, trial, preferred_element_type=F32)
    local = local + jnp.einsum(
        "vsij,sjk->vsik", trial_rows, right_block_ham, preferred_element_type=F32
    )

    pieces, mine, other, *strips = contract(target, trial, left_env, right_env)
    pieces = to_all(pieces, op)
    strips = [shift(strip, "x", k) for k, strip in enumerate(strips, 1)]
    others, hint = pack(strips)
    got = swap(other)

    (blocks,) = merge([hint, got], [pieces], sectors, False)
    dense, up, down = merge([blocks], [mine, got, *strips, swap(others)], sectors, True)
    blocks = to_all(blocks.reshape(nx, nz * here, 2, SUB, size), "x")
    for near in (3, 2, 1):
        up, down = shift(up, "z", 1), shift(down, "z", -1)
        up, down = join(dense, near, up), join(dense, 8 - near, down)
    up, down = shift(up, "z", 1), shift(down, "z", -1)
    halves = gate(reduce(blocks), up, down)
    second = to_all(halves.reshape(nz, here, 2, SUB, size), "z")
    parts = settle(dense, up, down)

    first = add(*(turn(parts[k], k) for k in range(RING)))

    scale = 1.0 / (sectors * size * size)
    hpsi, gram = finish(scale, first, second, local, trial_rows)
    gram = jnp.sum(spread(gram, ("y", "core")), axis=0)
    gram = jnp.sum(spread(gram, ("z", "x")), axis=0)
    return hpsi, gram


def solution(mesh):
    sizes = {"z": 8, "x": 4, "y": 4, "core": 2}
    fine = Mesh(mesh.devices.reshape(tuple(sizes.values())), tuple(sizes))
    sec, op = ("z", "x"), ("y", "core")
    return jax.shard_map(
        body,
        mesh=fine,
        in_specs=(
            P(None, sec, None, None),
            P(op, sec, None, None),
            P(op, sec, None, None),
            P(sec, op, None),
            P(sec, None, None),
            P(op, sec),
        ),
        out_specs=(P(None, sec, op, None), P()),
        check_vma=False,
    )
```
